32 devices in a mesh: fsdp: 8 (over y, x, core), tp: 4 (over z).
Axes of the slice: x: 2, y: 2, z: 4, core: 2. Of those that a mesh axis runs over, the one named last changes fastest.
Arguments:
- tokens: bfloat16 [4096, 4096], P(('fsdp', 'tp')), may hold values from -6 to 6
- in_weight: bfloat16 [4096, 3, 4096], P('fsdp', None, 'tp'), may hold values from -0.09375 to 0.09375
- out_weight: bfloat16 [4096, 4096], P('fsdp', 'tp'), may hold values from -0.09375 to 0.09375
- short_taps: float32 [3, 3, 4096], P(None, None, 'tp'), may hold values from -3 to 3
- filter_taps: float32 [128, 4096], P(None, 'tp'), may hold values from -1.2 to 1.2
- decay_rate: float32 [4096], P('tp'), may hold values from 0.00390625 to 0.09375
- doc_lengths: int32 [16], replicated, may hold values from 1 to 2048, 4096 in all
Outputs:
- mixed_out: bfloat16 [4096, 4096], P(('fsdp', 'tp'))
The draws below stay inside these ranges and needn't reach their ends.
Inputs may be any that keep to these rules, and one draw needn't show every extreme that they name: `doc_lengths`: the documents of the window in order; they sum to 4096.
All inputs are finite; a program needn't handle non-finite values.
Results may differ from the reference program's by a relative error of at most 0.014.
Values may be sent and summed in bfloat16 or wider, within the bound.
A program may use at most 128 MiB of HBM per device.

```python
import math
import jax
import jax.numpy as jnp
import numpy as np
from jax import lax

D = 4096
DW = 4096
FILT = 128
SLAB = 512
TOKENS = 4096
DOCS = 16
N_FSDP = 8


def level_of(key, extent, pieces, smallest, top_value):
    def one(position, parts):
        heights = jax.random.uniform(jax.random.fold_in(jax.random.fold_in(key, 6), position), (parts,), jnp.float32, smallest / len(pieces), top_value / len(pieces))
        return jnp.repeat(jnp.exp(heights), extent[position] // parts).reshape((-1,) + (1,) * (len(extent) - position - 1))

    factor_of = one(*pieces[0])
    for cut in pieces[1:]:
        factor_of = factor_of * one(*cut)
    return factor_of


def length_profile(count, total, bound, slope):
    loads = [(1 << 20) // math.isqrt(standing ** slope) + 1 for standing in range(2, count + 1)]
    rest, holding = total - bound - (count - 1), [1] * (count - 1)
    while rest > 0:
        free = [i for i in range(count - 1) if holding[i] < bound]
        whole, left = sum([loads[i] for i in free]), rest
        for i in free:
            addition = min(bound - holding[i], max(1, left * loads[i] // whole), rest)
            holding[i] = holding[i] + addition
            rest = rest - addition
    return np.array([bound] + holding)


def ragged(rng, count, total, bound, slope):
    if count == 2:
        one = jax.random.randint(rng, (), max(1, total - bound), min(bound, total - 1) + 1)
        return jnp.stack([one, total - one])
    sizes = jnp.asarray(length_profile(count, total, bound, slope), jnp.int32)
    pairs = (count - 1) // 2
    donor, sink = sizes[1:1 + 2 * pairs:2], sizes[2:2 + 2 * pairs:2]
    margin = jnp.minimum(donor - 1, bound - sink)
    shifted = jax.random.randint(jax.random.fold_in(rng, 1), (pairs,), 0, 1 << 20) % (margin + 1)
    sizes = sizes.at[1:1 + 2 * pairs:2].set(donor - shifted).at[2:2 + 2 * pairs:2].set(sink + shifted)
    return sizes[jax.random.permutation(jax.random.fold_in(rng, 2), count)]


def scatter_about(rng, dims, width, bound, pieces=(), held_as=jnp.bfloat16):
    factor_of = level_of(rng, dims, pieces, -0.22, 0.18) if pieces else 1.0
    entries = jax.random.normal(rng, dims, jnp.float32) * width * factor_of
    return jnp.minimum(jnp.maximum(entries, -bound), bound).astype(held_as)


def setup_inputs(seed: int = 0) -> dict:
    key_of = jax.random.split(jax.random.key(seed), 8)
    return {
        "tokens": scatter_about(key_of[0], (TOKENS, D), 1.0, 6.0, ((0, 32),)),
        "in_weight": scatter_about(key_of[1], (D, 3, DW), D ** -0.5, 0.09375, ((0, 8), (2, 4))),
        "out_weight": scatter_about(key_of[2], (D, DW), DW ** -0.5, 0.09375, ((0, 8), (1, 4))),
        "short_taps": scatter_about(key_of[3], (3, 3, DW), 0.6, 3.0, ((2, 4),), jnp.float32),
        "filter_taps": scatter_about(key_of[4], (FILT, DW), 0.2, 1.2, ((1, 4),), jnp.float32),
        "decay_rate": jnp.clip(jnp.exp(math.log(0.09375) - 3.1780538 * jax.random.uniform(key_of[5], (DW,), jnp.float32) ** level_of(key_of[5], (DW,), ((0, 4),), -0.2, 0.2)), 0.00390625, 0.09375),
        "doc_lengths": ragged(key_of[6], DOCS, TOKENS, 4 * SLAB, 2).astype(jnp.int32),
    }


def doc_position(points, lengths):
    starts = jnp.cumsum(lengths).astype(jnp.int32) - lengths
    begins = lax.optimization_barrier(jnp.max(jnp.where(starts[None, :] <= points[:, None], starts[None, :], 0), axis=1))
    return (points - begins).astype(jnp.int32)

def short_filter(extended, short_taps, positions, out_count):
    running = jnp.zeros((out_count,) + extended.shape[1:], jnp.float32)
    for tap_index in range(3):
        window = extended[2 - tap_index:2 - tap_index + out_count].astype(jnp.float32)
        inside = (positions >= tap_index)[:, None, None]
        running = running + jnp.where(inside, short_taps[tap_index][None] * window, jnp.float32(0.0))
    return running

def reference(tokens, in_weight, out_weight, short_taps, filter_taps, decay_rate, doc_lengths):
    widened = tokens.astype(jnp.float32)
    normed = (widened * lax.rsqrt(lax.optimization_barrier(jnp.mean(widened * widened, axis=1, keepdims=True)) + 1e-06)).astype(jnp.bfloat16)
    flat_in = in_weight.reshape(D, 3 * DW)
    blocks = normed.reshape(N_FSDP, SLAB, D)
    projected = lax.map(lambda block: jnp.dot(block, flat_in, preferred_element_type=jnp.float32).astype(jnp.bfloat16), blocks)
    projected = projected.reshape(TOKENS, 3, DW)
    points = jnp.arange(TOKENS, dtype=jnp.int32)
    positions = doc_position(points, doc_lengths)
    padded = jnp.concatenate([jnp.zeros((2, 3, DW), projected.dtype), projected], 0)
    short_out = short_filter(padded, short_taps, positions, TOKENS)
    kv_product = (short_out[:, 1] * short_out[:, 2]).astype(jnp.bfloat16)
    shaped = filter_taps * jnp.exp(-decay_rate[None, :] * jnp.arange(FILT, dtype=jnp.float32)[:, None])
    kv_padded = jnp.concatenate([jnp.zeros((FILT, DW), kv_product.dtype), kv_product], 0)

    def one_tap(tap_index, running):
        window = lax.dynamic_slice_in_dim(kv_padded, (FILT - tap_index).astype(jnp.int32), TOKENS, 0)
        weight_row = lax.dynamic_slice_in_dim(shaped, tap_index.astype(jnp.int32), 1, 0)
        inside = (positions >= tap_index)[:, None]
        return running + jnp.where(inside, weight_row * window.astype(jnp.float32), jnp.float32(0.0))
    long_mix = lax.fori_loop(0, FILT, one_tap, jnp.zeros((TOKENS, DW), jnp.float32))
    gated_mix = (short_out[:, 0] * long_mix).astype(jnp.bfloat16)
    outgoing = lax.dot_general(gated_mix, out_weight, (((1,), (1,)), ((), ())), preferred_element_type=jnp.float32)
    return (widened + outgoing).astype(jnp.bfloat16)
```

```python
import jax
import jax.numpy as jnp
from jax import lax
from jax.experimental import pallas as pl
from jax.experimental.pallas import tpu as pltpu
from jax.sharding import PartitionSpec as P

MESH = pl.DeviceIdType.MESH
HALO = 144


def doc_position(points, lengths):
    starts = jnp.cumsum(lengths) - lengths
    begins = jnp.max(jnp.where(starts[None, :] <= points[:, None], starts[None, :], 0), axis=1)
    return points - begins


def normalize(tokens):
    widened = tokens.astype(jnp.float32)
    return (
        widened * lax.rsqrt(jnp.mean(widened * widened, axis=1, keepdims=True) + 1e-06)
    ).astype(jnp.bfloat16)


def shape_filter(filter_taps, decay_rate):
    tap_count = filter_taps.shape[0]
    return filter_taps * jnp.exp(
        -decay_rate[None, :] * jnp.arange(tap_count, dtype=jnp.float32)[:, None]
    )


def from_behind(value, axis, by):
    length = lax.axis_size(axis)
    pairs = [(i, i + by) for i in range(length) if 0 <= i + by < length]
    return lax.ppermute(value, axis, pairs)


def short_filter(extended, short_taps, positions, out_count):
    running = jnp.zeros((out_count,) + extended.shape[1:], jnp.float32)
    for tap_index in range(3):
        window = extended[2 - tap_index : 2 - tap_index + out_count].astype(jnp.float32)
        inside = (positions >= tap_index)[:, None, None]
        running = running + jnp.where(
            inside, short_taps[tap_index][None] * window, jnp.float32(0.0)
        )
    return running


def long_filter(extended, shaped, positions, out_count, tap_count):
    def tap_group(group_index, running):
        for inner in range(16):
            tap_index = group_index * 16 + inner
            window = lax.dynamic_slice_in_dim(extended, tap_count - tap_index, out_count, 0)
            weight_row = lax.dynamic_slice_in_dim(shaped, tap_index, 1, 0)
            inside = (positions >= tap_index)[:, None]
            running = running + jnp.where(
                inside, weight_row * window.astype(jnp.float32), jnp.float32(0.0)
            )
        return running

    zero_sum = jnp.zeros((out_count, shaped.shape[1]), jnp.float32)
    return lax.fori_loop(0, tap_count // 16, tap_group, zero_sum)


def general_body(tokens, in_weight, out_weight, short_taps, filter_taps, decay_rate, doc_lengths):
    slab_count = tokens.shape[0] * lax.axis_size("tp")
    channels = in_weight.shape[2]
    tap_count = filter_taps.shape[0]
    gathered = lax.all_gather(normalize(tokens), "tp", axis=0, tiled=True)
    shard_piece = lax.all_gather(in_weight, "fsdp", axis=0, tiled=True)
    flat_piece = shard_piece.reshape(shard_piece.shape[0], 3 * channels)
    projected = jnp.dot(gathered, flat_piece, preferred_element_type=jnp.float32)
    out_full = lax.all_gather(out_weight, "fsdp", axis=0, tiled=True)
    projected = projected.astype(jnp.bfloat16).reshape(slab_count, 3, channels)
    first_row = lax.axis_index("fsdp") * slab_count
    own_points = first_row + jnp.arange(slab_count, dtype=jnp.int32)
    own_position = doc_position(own_points, doc_lengths)
    edge_rows = from_behind(projected[slab_count - 2 :], "fsdp", 1)
    short_all = short_filter(
        jnp.concatenate([edge_rows, projected], 0), short_taps, own_position, slab_count
    )
    kv_product = (short_all[:, 1] * short_all[:, 2]).astype(jnp.bfloat16)
    tail_rows = from_behind(kv_product[slab_count - tap_count :], "fsdp", 1)
    extended = jnp.concatenate([tail_rows, kv_product], 0)
    shaped = shape_filter(filter_taps, decay_rate)
    long_mix = long_filter(extended, shaped, own_position, slab_count, tap_count)
    gated_mix = (short_all[:, 0] * long_mix).astype(jnp.bfloat16)
    return finish(tokens, gated_mix, out_full)


def finish(tokens, gated_mix, out_full):
    summed = lax.psum_scatter(
        lax.dot_general(
            gated_mix, out_full, (((1,), (1,)), ((), ())), preferred_element_type=jnp.float32
        ).astype(jnp.bfloat16),
        "tp",
        scatter_dimension=0,
        tiled=True,
    ).astype(jnp.float32)
    return (tokens.astype(jnp.float32) + summed).astype(jnp.bfloat16)


def mix_kernel(
    x_ref, w_ref, o_ref, taps_ref, shaped_ref, pos_ref,
    gated_ref, ofull_ref,
    wbuf, xbuf, pbuf, fbuf, kvbuf, shbuf,
    wsend, wrecv, tsend, trecv, hsend, hrecv, lsem,
):
    chunks, depth, width = w_ref.shape
    cw = width // 3
    rows = x_ref.shape[0]
    f = lax.axis_index("fsdp")
    z = lax.axis_index("tp")
    nf = lax.axis_size("fsdp")
    nz = lax.axis_size("tp")
    slab = rows * nz
    half = depth // 2
    sib = f + 1 - 2 * lax.rem(f, 2)
    xn = f + 2 - 4 * lax.rem(f // 2, 2)
    yn = f + 4 - 8 * (f // 4)
    dn = f + 2 - 4 * lax.rem(f // 2, 2) + 4 - 8 * (f // 4)

    def other(core_of):
        return core_of + 1 - 2 * lax.rem(core_of, 2)

    xbuf[pl.ds(pl.multiple_of(z * rows, rows), rows), :] = x_ref[...]

    @pl.when(f == 0)
    def _():
        for k in range(chunks):
            pbuf[k, 0:HALO, :] = jnp.zeros((HALO, width), pbuf.dtype)

    barrier = pltpu.get_barrier_semaphore()
    for peer in (sib, xn, yn):
        pl.semaphore_signal(barrier, inc=1, device_id=(peer, z), device_id_type=MESH)

    @pl.when(z > 0)
    def _():
        pl.semaphore_signal(barrier, inc=1, device_id=(f, z - 1), device_id_type=MESH)

    @pl.when(z < nz - 1)
    def _():
        pl.semaphore_signal(barrier, inc=1, device_id=(f, z + 1), device_id_type=MESH)

    beside = f - 1 + 2 * lax.rem(f, 2)

    @pl.when(jnp.logical_and(beside >= 0, beside < nf))
    def _():
        pl.semaphore_signal(barrier, inc=1, device_id=(beside, z), device_id_type=MESH)

    peers = (
        3
        + (z + nz - 1) // nz
        + (2 * nz - 2 - z) // nz
        + (f + nf - 1) // nf
        + (2 * nf - 2 - f) // nf
        - 1
    )
    pl.semaphore_wait(barrier, peers)

    def own(p):
        return w_ref.at[p] if p < chunks else o_ref

    def slot(p, origin, part):
        start, size = ((0, depth), (0, half), (half, half))[part]
        at = pl.ds(pl.multiple_of(origin * depth + start, half), size)
        return wbuf.at[p, at] if p < chunks else ofull_ref.at[at]

    def move(p, number, source, origin, part, peer):
        return pltpu.make_async_remote_copy(
            src_ref=source,
            dst_ref=slot(p, origin, part),
            send_sem=wsend.at[p, number],
            recv_sem=wrecv.at[p, number],
            device_id=(peer, z),
            device_id_type=MESH,
        )

    def sends(p):
        return [
            move(p, 0, own(p), f, 0, xn),
            move(p, 1, own(p), f, 0, yn),
            move(p, 2, own(p), f, 0, sib),
            move(p, 3, slot(p, xn, 1), xn, 1, yn),
            move(p, 4, slot(p, yn, 2), yn, 2, xn),
            move(p, 5, slot(p, xn, 0), xn, 0, sib),
            move(p, 6, slot(p, yn, 0), yn, 0, sib),
            move(p, 7, slot(p, dn, 1), dn, 1, sib),
            move(p, 8, slot(p, dn, 2), dn, 2, sib),
        ]

    def arrivals(p):
        where = [
            (xn, 0), (yn, 0), (sib, 0), (dn, 1), (dn, 2),
            (other(xn), 0), (other(yn), 0), (other(dn), 1), (other(dn), 2),
        ]
        return [
            pltpu.make_async_remote_copy(
                src_ref=slot(p, origin, part),
                dst_ref=slot(p, origin, part),
                send_sem=wsend.at[p, number],
                recv_sem=wrecv.at[p, number],
                device_id=(sib, z),
                device_id_type=MESH,
            )
            for number, (origin, part) in enumerate(where)
        ]

    out = [sends(p) for p in range(chunks + 1)]
    come = [arrivals(p) for p in range(chunks + 1)]
    local = [
        pltpu.make_async_copy(own(p), slot(p, f, 0), lsem.at[p]) for p in range(chunks + 1)
    ]

    def launch(p):
        if p <= chunks:
            for number in (0, 1, 2):
                out[p][number].start()
            local[p].start()

    def spread(p):
        if p <= chunks:
            come[p][0].wait_recv()
            out[p][3].start()
            come[p][1].wait_recv()
            out[p][4].start()
            out[p][5].start()
            out[p][6].start()
            launch(p + 2)

    def spread_far(p):
        if p <= chunks:
            come[p][3].wait_recv()
            out[p][7].start()
            come[p][4].wait_recv()
            out[p][8].start()

    def ready(p):
        for number in (2, 5, 6, 7, 8):
            come[p][number].wait_recv()
        local[p].wait()

    def hop(way, step):
        origin = z - step if way == 0 else z + step
        at = pl.ds(pl.multiple_of(origin * rows, rows), rows)
        return pltpu.make_async_remote_copy(
            src_ref=xbuf.at[at],
            dst_ref=xbuf.at[at],
            send_sem=tsend.at[way, step],
            recv_sem=trecv.at[way, step],
            device_id=(f, z + 1 if way == 0 else z - 1),
            device_id_type=MESH,
        )

    def sends_hop(way, step):
        if way == 0:
            return jnp.logical_and(z - step >= 0, z < nz - 1)
        return jnp.logical_and(z + step <= nz - 1, z > 0)

    def gets_hop(way, step):
        return z - 1 - step >= 0 if way == 0 else z + 1 + step <= nz - 1

    def start_hop(step):
        for way in (0, 1):
            @pl.when(sends_hop(way, step))
            def _():
                hop(way, step).start()

    def end_hop(step):
        for way in (0, 1):
            @pl.when(gets_hop(way, step))
            def _():
                origin = z - 1 - step if way == 0 else z + 1 + step
                at = pl.ds(pl.multiple_of(origin * rows, rows), rows)
                pltpu.make_async_remote_copy(
                    src_ref=xbuf.at[at],
                    dst_ref=xbuf.at[at],
                    send_sem=tsend.at[way, step],
                    recv_sem=trecv.at[way, step],
                    device_id=(f, z + 1 if way == 1 else z - 1),
                    device_id_type=MESH,
                ).wait_recv()

    def project(k):
        @pl.loop(0, 3)
        def _(branch):
            at = pl.ds(pl.multiple_of(branch * cw, cw), cw)
            pbuf[k, HALO : HALO + slab, at] = jnp.dot(
                xbuf[...], wbuf[k, :, at], preferred_element_type=jnp.float32
            ).astype(pbuf.dtype)

    def halo(k):
        return pltpu.make_async_remote_copy(
            src_ref=pbuf.at[k, pl.ds(slab, HALO)],
            dst_ref=pbuf.at[k, pl.ds(0, HALO)],
            send_sem=hsend.at[k],
            recv_sem=hrecv.at[k],
            device_id=(f + 1, z),
            device_id_type=MESH,
        )

    def send_halo(k):
        @pl.when(f < nf - 1)
        def _():
            halo(k).start()

    def get_halo(k):
        @pl.when(f > 0)
        def _():
            halo(k).wait_recv()

    ext = slab + 128

    def convolve(k):
        @pl.loop(0, cw // 128)
        def _(lane):
            lanes = pl.ds(pl.multiple_of(k * cw + lane * 128, 128), 128)
            for branch in range(3):
                source = pl.ds(pl.multiple_of(branch * cw + lane * 128, 128), 128)
                fbuf[branch] = pbuf[k, :, source].astype(jnp.float32)

            def short(branch, first, count):
                total = jnp.zeros((count, 128), jnp.float32)
                place = pos_ref[pl.ds(first, count), :]
                for tap in range(3):
                    weight = taps_ref[pl.ds(tap * 3 + branch, 1), lanes]
                    window = fbuf[branch, pl.ds(first - tap, count), :]
                    total = total + jnp.where(place >= tap, weight * window, 0.0)
                return total

            for block in range(ext // 128):
                first = HALO - 128 + block * 128
                product = short(1, first, 128) * short(2, first, 128)
                kvbuf[pl.ds(block * 128, 128), :] = product.astype(jnp.bfloat16).astype(
                    jnp.float32
                )
            for shift in range(8):
                shbuf[shift, pl.ds(8, ext - 8), :] = kvbuf[pl.ds(8 - shift, ext - 8), :]

            for block in range(slab // 128):
                place = pos_ref[pl.ds(HALO + block * 128, 128), :]

                def taps(group, total):
                    weights = shaped_ref[pl.ds(pl.multiple_of(group * 8, 8), 8), lanes]
                    start = pl.multiple_of(128 + block * 128 - group * 8, 8)
                    for shift in range(8):
                        window = shbuf[shift, pl.ds(start, 128), :]
                        total = total + jnp.where(
                            place >= group * 8 + shift,
                            weights[shift : shift + 1, :] * window,
                            0.0,
                        )
                    return total

                mixed = lax.fori_loop(0, 16, taps, jnp.zeros((128, 128), jnp.float32))
                query = short(0, HALO + block * 128, 128)
                gated_ref[pl.ds(block * 128, 128), lanes] = (query * mixed).astype(
                    jnp.bfloat16
                )

    start_hop(0)
    launch(0)
    launch(1)
    spread(0)
    end_hop(0)
    start_hop(1)
    spread_far(0)
    spread(1)
    end_hop(1)
    start_hop(2)
    spread_far(1)
    spread(2)
    end_hop(2)
    ready(0)
    project(0)
    send_halo(0)
    spread_far(2)
    spread(3)
    ready(1)
    project(1)
    send_halo(1)
    spread_far(3)
    spread(4)
    get_halo(0)
    convolve(0)
    spread_far(4)
    for k in range(2, chunks):
        ready(k)
        project(k)
        send_halo(k)
        get_halo(k - 1)
        convolve(k - 1)
    get_halo(chunks - 1)
    convolve(chunks - 1)
    ready(chunks)

    for p in range(chunks + 1):
        for copy in out[p]:
            copy.wait_send()
    for step in range(3):
        for way in (0, 1):
            @pl.when(sends_hop(way, step))
            def _():
                hop(way, step).wait_send()

    @pl.when(f < nf - 1)
    def _():
        for k in range(chunks):
            halo(k).wait_send()


def body(tokens, in_weight, out_weight, short_taps, filter_taps, decay_rate, doc_lengths):
    rows, model = tokens.shape
    depth, _, channels = in_weight.shape
    slab = rows * lax.axis_size("tp")
    nf = lax.axis_size("fsdp")
    chunks = 4
    cw = channels // chunks
    normed = normalize(tokens)
    pieces = in_weight.reshape(depth, 3, chunks, cw).transpose(2, 0, 1, 3).reshape(
        chunks, depth, 3 * cw
    )
    points = (
        lax.axis_index("fsdp") * slab - HALO + jnp.arange(slab + HALO, dtype=jnp.int32)
    )
    position = jnp.broadcast_to(doc_position(points, doc_lengths)[:, None], (slab + HALO, 128))
    shaped = shape_filter(filter_taps, decay_rate)
    vmem = pl.BlockSpec(memory_space=pltpu.VMEM)
    anywhere = pl.BlockSpec(memory_space=pl.ANY)
    gated, out_full = pl.pallas_call(
        mix_kernel,
        out_shape=(
            jax.ShapeDtypeStruct((slab, channels), jnp.bfloat16),
            jax.ShapeDtypeStruct((nf * depth, channels), jnp.bfloat16),
        ),
        in_specs=[vmem, anywhere, anywhere, vmem, vmem, vmem],
        out_specs=(vmem, anywhere),
        scratch_shapes=[
            pltpu.VMEM((chunks, nf * depth, 3 * cw), jnp.bfloat16),
            pltpu.VMEM((slab, model), jnp.bfloat16),
            pltpu.VMEM((chunks, slab + HALO, 3 * cw), jnp.bfloat16),
            pltpu.VMEM((3, slab + HALO, 128), jnp.float32),
            pltpu.VMEM((slab + 128, 128), jnp.float32),
            pltpu.VMEM((8, slab + 128, 128), jnp.float32),
            pltpu.SemaphoreType.DMA((chunks + 1, 9)),
            pltpu.SemaphoreType.DMA((chunks + 1, 9)),
            pltpu.SemaphoreType.DMA((2, 3)),
            pltpu.SemaphoreType.DMA((2, 3)),
            pltpu.SemaphoreType.DMA((chunks,)),
            pltpu.SemaphoreType.DMA((chunks,)),
            pltpu.SemaphoreType.DMA((chunks + 1,)),
        ],
        compiler_params=pltpu.CompilerParams(
            collective_id=0, has_side_effects=True, vmem_limit_bytes=56 * 1024 * 1024
        ),
        cost_estimate=pl.CostEstimate(
            flops=2 * slab * model * 3 * channels,
            bytes_accessed=64 * 1024 * 1024,
            transcendentals=0,
        ),
    )(normed, pieces, out_weight, short_taps.reshape(9, channels), shaped, position)
    return finish(tokens, gated, out_full)


def solution(mesh):
    in_specs = (
        P(("fsdp", "tp"), None),
        P("fsdp", None, "tp"),
        P("fsdp", "tp"),
        P(None, None, "tp"),
        P(None, "tp"),
        P("tp"),
        P(),
    )
    out_specs = P(("fsdp", "tp"), None)
    small = mesh.shape["fsdp"] == 8 and mesh.shape["tp"] == 4
    return jax.shard_map(
        body if small else general_body,
        mesh=mesh,
        in_specs=in_specs,
        out_specs=out_specs,
        check_vma=False,
    )
```

```python
import jax
import jax.numpy as jnp
from jax import lax
from jax.experimental import pallas as pl
from jax.experimental.pallas import tpu as pltpu
from jax.sharding import PartitionSpec as P

MESH = pl.DeviceIdType.MESH
HALO = 144


def doc_position(points, lengths):
    starts = jnp.cumsum(lengths) - lengths
    begins = jnp.max(jnp.where(starts[None, :] <= points[:, None], starts[None, :], 0), axis=1)
    return points - begins


def normalize(tokens):
    widened = tokens.astype(jnp.float32)
    return (
        widened * lax.rsqrt(jnp.mean(widened * widened, axis=1, keepdims=True) + 1e-06)
    ).astype(jnp.bfloat16)


def shape_filter(filter_taps, decay_rate):
    tap_count = filter_taps.shape[0]
    return filter_taps * jnp.exp(
        -decay_rate[None, :] * jnp.arange(tap_count, dtype=jnp.float32)[:, None]
    )


def from_behind(value, axis, by):
    length = lax.axis_size(axis)
    pairs = [(i, i + by) for i in range(length) if 0 <= i + by < length]
    return lax.ppermute(value, axis, pairs)


def short_filter(extended, short_taps, positions, out_count):
    running = jnp.zeros((out_count,) + extended.shape[1:], jnp.float32)
    for tap_index in range(3):
        window = extended[2 - tap_index : 2 - tap_index + out_count].astype(jnp.float32)
        inside = (positions >= tap_index)[:, None, None]
        running = running + jnp.where(
            inside, short_taps[tap_index][None] * window, jnp.float32(0.0)
        )
    return running


def long_filter(extended, shaped, positions, out_count, tap_count):
    def tap_group(group_index, running):
        for inner in range(16):
            tap_index = group_index * 16 + inner
            window = lax.dynamic_slice_in_dim(extended, tap_count - tap_index, out_count, 0)
            weight_row = lax.dynamic_slice_in_dim(shaped, tap_index, 1, 0)
            inside = (positions >= tap_index)[:, None]
            running = running + jnp.where(
                inside, weight_row * window.astype(jnp.float32), jnp.float32(0.0)
            )
        return running

    zero_sum = jnp.zeros((out_count, shaped.shape[1]), jnp.float32)
    return lax.fori_loop(0, tap_count // 16, tap_group, zero_sum)


def general_body(tokens, in_weight, out_weight, short_taps, filter_taps, decay_rate, doc_lengths):
    slab_count = tokens.shape[0] * lax.axis_size("tp")
    channels = in_weight.shape[2]
    tap_count = filter_taps.shape[0]
    gathered = lax.all_gather(normalize(tokens), "tp", axis=0, tiled=True)
    shard_piece = lax.all_gather(in_weight, "fsdp", axis=0, tiled=True)
    flat_piece = shard_piece.reshape(shard_piece.shape[0], 3 * channels)
    projected = jnp.dot(gathered, flat_piece, preferred_element_type=jnp.float32)
    out_full = lax.all_gather(out_weight, "fsdp", axis=0, tiled=True)
    projected = projected.astype(jnp.bfloat16).reshape(slab_count, 3, channels)
    first_row = lax.axis_index("fsdp") * slab_count
    own_points = first_row + jnp.arange(slab_count, dtype=jnp.int32)
    own_position = doc_position(own_points, doc_lengths)
    edge_rows = from_behind(projected[slab_count - 2 :], "fsdp", 1)
    short_all = short_filter(
        jnp.concatenate([edge_rows, projected], 0), short_taps, own_position, slab_count
    )
    kv_product = (short_all[:, 1] * short_all[:, 2]).astype(jnp.bfloat16)
    tail_rows = from_behind(kv_product[slab_count - tap_count :], "fsdp", 1)
    extended = jnp.concatenate([tail_rows, kv_product], 0)
    shaped = shape_filter(filter_taps, decay_rate)
    long_mix = long_filter(extended, shaped, own_position, slab_count, tap_count)
    gated_mix = (short_all[:, 0] * long_mix).astype(jnp.bfloat16)
    return finish(tokens, gated_mix, out_full)


def finish(tokens, gated_mix, out_full):
    summed = lax.psum_scatter(
        lax.dot_general(
            gated_mix, out_full, (((1,), (1,)), ((), ())), preferred_element_type=jnp.float32
        ).astype(jnp.bfloat16),
        "tp",
        scatter_dimension=0,
        tiled=True,
    ).astype(jnp.float32)
    return (tokens.astype(jnp.float32) + summed).astype(jnp.bfloat16)


def mix_kernel(
    len_ref, x_ref, w_ref, o_ref, taps_ref, filter_ref, decay_ref,
    out_ref,
    gated_ref, ofull_ref, shaped_ref, pos_ref,
    wbuf, xbuf, pbuf, fbuf, kvbuf, shbuf, rbuf, sums,
    wsend, wrecv, tsend, trecv, hsend, hrecv, lsem, rsend, rrecv,
):
    depth = w_ref.shape[1]
    chunks, _, width = wbuf.shape
    cw = width // 3
    tap_count = filter_ref.shape[0]
    rows = x_ref.shape[0]
    f = lax.axis_index("fsdp")
    z = lax.axis_index("tp")
    nf = lax.axis_size("fsdp")
    nz = lax.axis_size("tp")
    slab = rows * nz
    half = depth // 2
    sib = f + 1 - 2 * lax.rem(f, 2)
    xn = f + 2 - 4 * lax.rem(f // 2, 2)
    yn = f + 4 - 8 * (f // 4)
    dn = f + 2 - 4 * lax.rem(f // 2, 2) + 4 - 8 * (f // 4)

    def other(core_of):
        return core_of + 1 - 2 * lax.rem(core_of, 2)

    @pl.loop(0, rows // 16)
    def _(group):
        at = pl.ds(pl.multiple_of(group * 16, 16), 16)
        put = pl.ds(pl.multiple_of(z * rows + group * 16, 16), 16)
        xbuf[put, :] = normalize(x_ref[at, :])

    for first in range(0, HALO + slab, 16):
        point = f * slab - HALO + first + lax.broadcasted_iota(jnp.int32, (16, 128), 0)
        start = jnp.int32(0)
        begins = jnp.zeros((16, 128), jnp.int32)
        for doc in range(len_ref.shape[0]):
            begins = jnp.maximum(begins, jnp.where(start <= point, start, 0))
            start = start + len_ref[doc]
        pos_ref[first : first + 16, :] = point - begins

    @pl.loop(0, tap_count // 8)
    def _(group):
        at = pl.ds(pl.multiple_of(group * 8, 8), 8)
        tap = (group * 8 + lax.broadcasted_iota(jnp.int32, (8, decay_ref.shape[1]), 0)).astype(
            jnp.float32
        )
        shaped_ref[at, :] = filter_ref[at, :] * jnp.exp(-decay_ref[...] * tap)

    @pl.when(f == 0)
    def _():
        for k in range(chunks):
            pbuf[k, 0:HALO, :] = jnp.zeros((HALO, width), pbuf.dtype)

    mine = pl.ds(pl.multiple_of(f * depth, depth), depth)
    local = [
        [
            pltpu.make_async_copy(
                w_ref.at[branch, :, pl.ds(p * cw, cw)],
                wbuf.at[p, mine, pl.ds(branch * cw, cw)],
                lsem.at[p, branch],
            )
            for branch in range(3)
        ]
        for p in range(chunks)
    ] + [[pltpu.make_async_copy(o_ref, ofull_ref.at[mine], lsem.at[chunks, 0])]]
    for piece in local:
        for copy in piece:
            copy.start()

    barrier = pltpu.get_barrier_semaphore()
    for peer in (sib, xn, yn):
        pl.semaphore_signal(barrier, inc=1, device_id=(peer, z), device_id_type=MESH)

    @pl.when(z > 0)
    def _():
        pl.semaphore_signal(barrier, inc=1, device_id=(f, z - 1), device_id_type=MESH)

    @pl.when(z < nz - 1)
    def _():
        pl.semaphore_signal(barrier, inc=1, device_id=(f, z + 1), device_id_type=MESH)

    beside = f - 1 + 2 * lax.rem(f, 2)

    @pl.when(jnp.logical_and(beside >= 0, beside < nf))
    def _():
        pl.semaphore_signal(barrier, inc=1, device_id=(beside, z), device_id_type=MESH)

    peers = (
        3
        + (z + nz - 1) // nz
        + (2 * nz - 2 - z) // nz
        + (f + nf - 1) // nf
        + (2 * nf - 2 - f) // nf
        - 1
    )
    pl.semaphore_wait(barrier, peers)

    def slot(p, origin, part):
        start, size = ((0, depth), (0, half), (half, half))[part]
        at = pl.ds(pl.multiple_of(origin * depth + start, half), size)
        return wbuf.at[p, at] if p < chunks else ofull_ref.at[at]

    def move(p, number, source, origin, part, peer):
        return pltpu.make_async_remote_copy(
            src_ref=source,
            dst_ref=slot(p, origin, part),
            send_sem=wsend.at[p, number],
            recv_sem=wrecv.at[p, number],
            device_id=(peer, z),
            device_id_type=MESH,
        )

    def sends(p):
        return [
            move(p, 0, slot(p, f, 0), f, 0, xn),
            move(p, 1, slot(p, f, 0), f, 0, yn),
            move(p, 2, slot(p, f, 0), f, 0, sib),
            move(p, 3, slot(p, xn, 1), xn, 1, yn),
            move(p, 4, slot(p, yn, 2), yn, 2, xn),
            move(p, 5, slot(p, xn, 0), xn, 0, sib),
            move(p, 6, slot(p, yn, 0), yn, 0, sib),
            move(p, 7, slot(p, dn, 1), dn, 1, sib),
            move(p, 8, slot(p, dn, 2), dn, 2, sib),
        ]

    def arrivals(p):
        where = [
            (xn, 0), (yn, 0), (sib, 0), (dn, 1), (dn, 2),
            (other(xn), 0), (other(yn), 0), (other(dn), 1), (other(dn), 2),
        ]
        return [
            pltpu.make_async_remote_copy(
                src_ref=slot(p, origin, part),
                dst_ref=slot(p, origin, part),
                send_sem=wsend.at[p, number],
                recv_sem=wrecv.at[p, number],
                device_id=(sib, z),
                device_id_type=MESH,
            )
            for number, (origin, part) in enumerate(where)
        ]

    out = [sends(p) for p in range(chunks + 1)]
    come = [arrivals(p) for p in range(chunks + 1)]

    def launch(p):
        if p <= chunks:
            for copy in local[p]:
                copy.wait()
            for number in (0, 1, 2):
                out[p][number].start()

    def spread(p):
        if p <= chunks:
            come[p][0].wait_recv()
            out[p][3].start()
            come[p][1].wait_recv()
            out[p][4].start()
            out[p][5].start()
            out[p][6].start()
            launch(p + 2)

    def spread_far(p):
        if p <= chunks:
            come[p][3].wait_recv()
            out[p][7].start()
            come[p][4].wait_recv()
            out[p][8].start()

    def ready(p):
        for number in (2, 5, 6, 7, 8):
            come[p][number].wait_recv()

    def hop(way, step):
        origin = z - step if way == 0 else z + step
        at = pl.ds(pl.multiple_of(origin * rows, rows), rows)
        return pltpu.make_async_remote_copy(
            src_ref=xbuf.at[at],
            dst_ref=xbuf.at[at],
            send_sem=tsend.at[way, step],
            recv_sem=trecv.at[way, step],
            device_id=(f, z + 1 if way == 0 else z - 1),
            device_id_type=MESH,
        )

    def sends_hop(way, step):
        if way == 0:
            return jnp.logical_and(z - step >= 0, z < nz - 1)
        return jnp.logical_and(z + step <= nz - 1, z > 0)

    def gets_hop(way, step):
        return z - 1 - step >= 0 if way == 0 else z + 1 + step <= nz - 1

    def start_hop(step):
        for way in (0, 1):
            @pl.when(sends_hop(way, step))
            def _():
                hop(way, step).start()

    def end_hop(step):
        for way in (0, 1):
            @pl.when(gets_hop(way, step))
            def _():
                origin = z - 1 - step if way == 0 else z + 1 + step
                at = pl.ds(pl.multiple_of(origin * rows, rows), rows)
                pltpu.make_async_remote_copy(
                    src_ref=xbuf.at[at],
                    dst_ref=xbuf.at[at],
                    send_sem=tsend.at[way, step],
                    recv_sem=trecv.at[way, step],
                    device_id=(f, z + 1 if way == 1 else z - 1),
                    device_id_type=MESH,
                ).wait_recv()

    def project(k):
        @pl.loop(0, 3)
        def _(branch):
            at = pl.ds(pl.multiple_of(branch * cw, cw), cw)
            pbuf[k, HALO : HALO + slab, at] = jnp.dot(
                xbuf[...], wbuf[k, :, at], preferred_element_type=jnp.float32
            ).astype(pbuf.dtype)

    def halo(k):
        return pltpu.make_async_remote_copy(
            src_ref=pbuf.at[k, pl.ds(slab, HALO)],
            dst_ref=pbuf.at[k, pl.ds(0, HALO)],
            send_sem=hsend.at[k],
            recv_sem=hrecv.at[k],
            device_id=(f + 1, z),
            device_id_type=MESH,
        )

    def send_halo(k):
        @pl.when(f < nf - 1)
        def _():
            halo(k).start()

    def get_halo(k):
        @pl.when(f > 0)
        def _():
            halo(k).wait_recv()

    ext = slab + 128

    def convolve(k):
        @pl.loop(0, cw // 128)
        def _(lane):
            lanes = pl.ds(pl.multiple_of(k * cw + lane * 128, 128), 128)
            for branch in range(3):
                source = pl.ds(pl.multiple_of(branch * cw + lane * 128, 128), 128)
                fbuf[branch] = pbuf[k, :, source].astype(jnp.float32)

            def short(branch, first, count):
                total = jnp.zeros((count, 128), jnp.float32)
                place = pos_ref[pl.ds(first, count), :]
                for tap in range(3):
                    weight = taps_ref[tap, pl.ds(branch, 1), lanes]
                    window = fbuf[branch, pl.ds(first - tap, count), :]
                    total = total + jnp.where(place >= tap, weight * window, 0.0)
                return total

            for block in range(ext // 128):
                first = HALO - 128 + block * 128
                product = short(1, first, 128) * short(2, first, 128)
                kvbuf[pl.ds(block * 128, 128), :] = product.astype(jnp.bfloat16).astype(
                    jnp.float32
                )
            for shift in range(8):
                shbuf[shift, pl.ds(8, ext - 8), :] = kvbuf[pl.ds(8 - shift, ext - 8), :]

            for block in range(slab // 128):
                place = pos_ref[pl.ds(HALO + block * 128, 128), :]

                def taps(group, total):
                    weights = shaped_ref[pl.ds(pl.multiple_of(group * 8, 8), 8), lanes]
                    start = pl.multiple_of(128 + block * 128 - group * 8, 8)
                    for shift in range(8):
                        window = shbuf[shift, pl.ds(start, 128), :]
                        total = total + jnp.where(
                            place >= group * 8 + shift,
                            weights[shift : shift + 1, :] * window,
                            0.0,
                        )
                    return total

                mixed = lax.fori_loop(0, 16, taps, jnp.zeros((128, 128), jnp.float32))
                query = short(0, HALO + block * 128, 128)
                gated_ref[pl.ds(block * 128, 128), lanes] = (query * mixed).astype(
                    jnp.bfloat16
                )

    columns = 2 * depth
    pairs = [f // 2, xn // 2, yn // 2, dn // 2]

    def part(owner, q):
        at = pl.ds(pl.multiple_of(pairs[q] * columns, columns), columns)
        return lax.dot_general(
            gated_ref[pl.ds(pl.multiple_of(owner * rows, rows), rows), :],
            ofull_ref[at, :],
            (((1,), (1,)), ((), ())),
            preferred_element_type=jnp.float32,
        )

    def carry(way, step, q):
        return pltpu.make_async_remote_copy(
            src_ref=rbuf.at[way, step, q],
            dst_ref=rbuf.at[way, step, q],
            send_sem=rsend.at[way, step, q],
            recv_sem=rrecv.at[way, step, q],
            device_id=(f, z + 1 if way == 0 else z - 1),
            device_id_type=MESH,
        )

    def arrive(way, step, q):
        pltpu.make_async_remote_copy(
            src_ref=rbuf.at[way, step, q],
            dst_ref=rbuf.at[way, step, q],
            send_sem=rsend.at[way, step, q],
            recv_sem=rrecv.at[way, step, q],
            device_id=(f, z - 1 if way == 0 else z + 1),
            device_id_type=MESH,
        ).wait_recv()

    def carries(way, step):
        return nz - 1 - step > z if way == 0 else step < z

    def has_before(way):
        return z > 0 if way == 0 else z < nz - 1

    def pass_sums(q):
        for step in range(3):
            for way in (0, 1):
                owner = 3 - step if way == 0 else step

                @pl.when(carries(way, step))
                def _():
                    value = part(owner, q)

                    @pl.when(has_before(way))
                    def _():
                        arrive(way, step, q)
                        rbuf[way, step, q] = (
                            value + rbuf[way, step, q].astype(jnp.float32)
                        ).astype(jnp.bfloat16)

                    @pl.when(jnp.logical_not(has_before(way)))
                    def _():
                        rbuf[way, step, q] = value.astype(jnp.bfloat16)

                    carry(way, step, q).start()

    def settle(q):
        at = pl.ds(pl.multiple_of(pairs[q] * columns, columns), columns)
        sums[...] = part(z, q) + x_ref[:, at].astype(jnp.float32)
        for step in range(3):
            for way in (0, 1):
                here = z == nz - 1 - step if way == 0 else z == step

                @pl.when(here)
                def _():
                    arrive(way, step, q)
                    sums[...] = sums[...] + rbuf[way, step, q].astype(jnp.float32)

        out_ref[:, at] = sums[...].astype(jnp.bfloat16)

    start_hop(0)
    launch(0)
    launch(1)
    spread(0)
    end_hop(0)
    start_hop(1)
    spread_far(0)
    spread(1)
    end_hop(1)
    start_hop(2)
    spread_far(1)
    spread(2)
    end_hop(2)
    ready(0)
    project(0)
    send_halo(0)
    spread_far(2)
    ready(1)
    project(1)
    send_halo(1)
    get_halo(0)
    convolve(0)
    spread(3)
    ready(2)
    project(2)
    send_halo(2)
    get_halo(1)
    convolve(1)
    spread_far(3)
    ready(3)
    project(3)
    send_halo(3)
    get_halo(2)
    convolve(2)
    spread(4)
    get_halo(3)
    convolve(3)
    come[chunks][2].wait_recv()
    pass_sums(0)
    spread_far(4)
    come[chunks][5].wait_recv()
    pass_sums(1)
    settle(0)
    come[chunks][6].wait_recv()
    pass_sums(2)
    settle(1)
    come[chunks][7].wait_recv()
    come[chunks][8].wait_recv()
    pass_sums(3)
    settle(2)
    settle(3)

    for step in range(3):
        for way in (0, 1):
            @pl.when(carries(way, step))
            def _():
                for q in range(4):
                    carry(way, step, q).wait_send()

    for p in range(chunks + 1):
        for copy in out[p]:
            copy.wait_send()
    for step in range(3):
        for way in (0, 1):
            @pl.when(sends_hop(way, step))
            def _():
                hop(way, step).wait_send()

    @pl.when(f < nf - 1)
    def _():
        for k in range(chunks):
            halo(k).wait_send()


def body(tokens, in_weight, out_weight, short_taps, filter_taps, decay_rate, doc_lengths):
    rows, model = tokens.shape
    depth, _, channels = in_weight.shape
    slab = rows * lax.axis_size("tp")
    nf = lax.axis_size("fsdp")
    chunks = 4
    cw = channels // chunks
    vmem = pl.BlockSpec(memory_space=pltpu.VMEM)
    anywhere = pl.BlockSpec(memory_space=pl.ANY)
    return pl.pallas_call(
        mix_kernel,
        out_shape=jax.ShapeDtypeStruct((rows, model), jnp.bfloat16),
        in_specs=[
            pl.BlockSpec(memory_space=pltpu.SMEM), vmem, anywhere, anywhere, vmem, vmem, vmem,
        ],
        out_specs=vmem,
        scratch_shapes=[
            pltpu.VMEM((slab, channels), jnp.bfloat16),
            pltpu.VMEM((nf * depth, channels), jnp.bfloat16),
            pltpu.VMEM(filter_taps.shape, jnp.float32),
            pltpu.VMEM((slab + HALO, 128), jnp.int32),
            pltpu.VMEM((chunks, nf * depth, 3 * cw), jnp.bfloat16),
            pltpu.VMEM((slab, model), jnp.bfloat16),
            pltpu.VMEM((chunks, slab + HALO, 3 * cw), jnp.bfloat16),
            pltpu.VMEM((3, slab + HALO, 128), jnp.float32),
            pltpu.VMEM((slab + 128, 128), jnp.float32),
            pltpu.VMEM((8, slab + 128, 128), jnp.float32),
            pltpu.VMEM((2, 3, 4, rows, 2 * depth), jnp.bfloat16),
            pltpu.VMEM((rows, 2 * depth), jnp.float32),
            pltpu.SemaphoreType.DMA((chunks + 1, 9)),
            pltpu.SemaphoreType.DMA((chunks + 1, 9)),
            pltpu.SemaphoreType.DMA((2, 3)),
            pltpu.SemaphoreType.DMA((2, 3)),
            pltpu.SemaphoreType.DMA((chunks,)),
            pltpu.SemaphoreType.DMA((chunks,)),
            pltpu.SemaphoreType.DMA((chunks + 1, 3)),
            pltpu.SemaphoreType.DMA((2, 3, 4)),
            pltpu.SemaphoreType.DMA((2, 3, 4)),
        ],
        compiler_params=pltpu.CompilerParams(
            collective_id=0, has_side_effects=True, vmem_limit_bytes=62 * 1024 * 1024
        ),
        cost_estimate=pl.CostEstimate(
            flops=2 * slab * model * 4 * channels,
            bytes_accessed=16 * 1024 * 1024,
            transcendentals=0,
        ),
    )(
        doc_lengths,
        tokens,
        in_weight.transpose(1, 0, 2),
        out_weight,
        short_taps,
        filter_taps,
        decay_rate[None, :],
    )


def solution(mesh):
    in_specs = (
        P(("fsdp", "tp"), None),
        P("fsdp", None, "tp"),
        P("fsdp", "tp"),
        P(None, None, "tp"),
        P(None, "tp"),
        P("tp"),
        P(),
    )
    out_specs = P(("fsdp", "tp"), None)
    small = mesh.shape["fsdp"] == 8 and mesh.shape["tp"] == 4
    return jax.shard_map(
        body if small else general_body,
        mesh=mesh,
        in_specs=in_specs,
        out_specs=out_specs,
        check_vma=False,
    )
```

```python
import jax
import jax.numpy as jnp
from jax import lax
from jax.experimental import pallas as pl
from jax.experimental.pallas import tpu as pltpu
from jax.sharding import PartitionSpec as P

MESH = pl.DeviceIdType.MESH
HALO = 144


def doc_position(points, lengths):
    starts = jnp.cumsum(lengths) - lengths
    begins = jnp.max(jnp.where(starts[None, :] <= points[:, None], starts[None, :], 0), axis=1)
    return points - begins


def normalize(tokens):
    widened = tokens.astype(jnp.float32)
    return (
        widened * lax.rsqrt(jnp.mean(widened * widened, axis=1, keepdims=True) + 1e-06)
    ).astype(jnp.bfloat16)


def shape_filter(filter_taps, decay_rate):
    tap_count = filter_taps.shape[0]
    return filter_taps * jnp.exp(
        -decay_rate[None, :] * jnp.arange(tap_count, dtype=jnp.float32)[:, None]
    )


def from_behind(value, axis, by):
    length = lax.axis_size(axis)
    pairs = [(i, i + by) for i in range(length) if 0 <= i + by < length]
    return lax.ppermute(value, axis, pairs)


def short_filter(extended, short_taps, positions, out_count):
    running = jnp.zeros((out_count,) + extended.shape[1:], jnp.float32)
    for tap_index in range(3):
        window = extended[2 - tap_index : 2 - tap_index + out_count].astype(jnp.float32)
        inside = (positions >= tap_index)[:, None, None]
        running = running + jnp.where(
            inside, short_taps[tap_index][None] * window, jnp.float32(0.0)
        )
    return running


def long_filter(extended, shaped, positions, out_count, tap_count):
    def tap_group(group_index, running):
        for inner in range(16):
            tap_index = group_index * 16 + inner
            window = lax.dynamic_slice_in_dim(extended, tap_count - tap_index, out_count, 0)
            weight_row = lax.dynamic_slice_in_dim(shaped, tap_index, 1, 0)
            inside = (positions >= tap_index)[:, None]
            running = running + jnp.where(
                inside, weight_row * window.astype(jnp.float32), jnp.float32(0.0)
            )
        return running

    zero_sum = jnp.zeros((out_count, shaped.shape[1]), jnp.float32)
    return lax.fori_loop(0, tap_count // 16, tap_group, zero_sum)


def general_body(tokens, in_weight, out_weight, short_taps, filter_taps, decay_rate, doc_lengths):
    slab_count = tokens.shape[0] * lax.axis_size("tp")
    channels = in_weight.shape[2]
    tap_count = filter_taps.shape[0]
    gathered = lax.all_gather(normalize(tokens), "tp", axis=0, tiled=True)
    shard_piece = lax.all_gather(in_weight, "fsdp", axis=0, tiled=True)
    flat_piece = shard_piece.reshape(shard_piece.shape[0], 3 * channels)
    projected = jnp.dot(gathered, flat_piece, preferred_element_type=jnp.float32)
    out_full = lax.all_gather(out_weight, "fsdp", axis=0, tiled=True)
    projected = projected.astype(jnp.bfloat16).reshape(slab_count, 3, channels)
    first_row = lax.axis_index("fsdp") * slab_count
    own_points = first_row + jnp.arange(slab_count, dtype=jnp.int32)
    own_position = doc_position(own_points, doc_lengths)
    edge_rows = from_behind(projected[slab_count - 2 :], "fsdp", 1)
    short_all = short_filter(
        jnp.concatenate([edge_rows, projected], 0), short_taps, own_position, slab_count
    )
    kv_product = (short_all[:, 1] * short_all[:, 2]).astype(jnp.bfloat16)
    tail_rows = from_behind(kv_product[slab_count - tap_count :], "fsdp", 1)
    extended = jnp.concatenate([tail_rows, kv_product], 0)
    shaped = shape_filter(filter_taps, decay_rate)
    long_mix = long_filter(extended, shaped, own_position, slab_count, tap_count)
    gated_mix = (short_all[:, 0] * long_mix).astype(jnp.bfloat16)
    return finish(tokens, gated_mix, out_full)


def finish(tokens, gated_mix, out_full):
    summed = lax.psum_scatter(
        lax.dot_general(
            gated_mix, out_full, (((1,), (1,)), ((), ())), preferred_element_type=jnp.float32
        ).astype(jnp.bfloat16),
        "tp",
        scatter_dimension=0,
        tiled=True,
    ).astype(jnp.float32)
    return (tokens.astype(jnp.float32) + summed).astype(jnp.bfloat16)


def mix_kernel(
    len_ref, x_ref, w_ref, o_ref, taps_ref, filter_ref, decay_ref,
    out_ref,
    gated_ref, ofull_ref, shaped_ref, pos_ref,
    wbuf, xbuf, pbuf, fbuf, kvbuf, shbuf, rbuf, sums,
    wsend, wrecv, tsend, trecv, hsend, hrecv, lsem, rsend, rrecv,
):
    depth = w_ref.shape[1]
    chunks, _, width = wbuf.shape
    cw = width // 3
    tap_count = filter_ref.shape[0]
    rows = x_ref.shape[0]
    f = lax.axis_index("fsdp")
    z = lax.axis_index("tp")
    nf = lax.axis_size("fsdp")
    nz = lax.axis_size("tp")
    slab = rows * nz
    half = depth // 2
    sib = f + 1 - 2 * lax.rem(f, 2)
    xn = f + 2 - 4 * lax.rem(f // 2, 2)
    yn = f + 4 - 8 * (f // 4)
    dn = f + 2 - 4 * lax.rem(f // 2, 2) + 4 - 8 * (f // 4)

    def other(core_of):
        return core_of + 1 - 2 * lax.rem(core_of, 2)

    @pl.loop(0, rows // 16)
    def _(group):
        at = pl.ds(pl.multiple_of(group * 16, 16), 16)
        put = pl.ds(pl.multiple_of(z * rows + group * 16, 16), 16)
        xbuf[put, :] = normalize(x_ref[at, :])

    for first in range(0, HALO + slab, 16):
        point = f * slab - HALO + first + lax.broadcasted_iota(jnp.int32, (16, 128), 0)
        start = jnp.int32(0)
        begins = jnp.zeros((16, 128), jnp.int32)
        for doc in range(len_ref.shape[0]):
            begins = jnp.maximum(begins, jnp.where(start <= point, start, 0))
            start = start + len_ref[doc]
        pos_ref[first : first + 16, :] = point - begins

    @pl.loop(0, tap_count // 8)
    def _(group):
        at = pl.ds(pl.multiple_of(group * 8, 8), 8)
        tap = (group * 8 + lax.broadcasted_iota(jnp.int32, (8, decay_ref.shape[1]), 0)).astype(
            jnp.float32
        )
        shaped_ref[at, :] = filter_ref[at, :] * jnp.exp(-decay_ref[...] * tap)

    @pl.when(f == 0)
    def _():
        for k in range(chunks):
            pbuf[k, 0:HALO, :] = jnp.zeros((HALO, width), pbuf.dtype)

    mine = pl.ds(pl.multiple_of(f * depth, depth), depth)
    local = [
        [
            pltpu.make_async_copy(
                w_ref.at[branch, :, pl.ds(p * cw, cw)],
                wbuf.at[p, mine, pl.ds(branch * cw, cw)],
                lsem.at[p, branch],
            )
            for branch in range(3)
        ]
        for p in range(chunks)
    ] + [[pltpu.make_async_copy(o_ref, ofull_ref.at[mine], lsem.at[chunks, 0])]]
    for piece in local:
        for copy in piece:
            copy.start()

    barrier = pltpu.get_barrier_semaphore()
    for peer in (sib, xn, yn):
        pl.semaphore_signal(barrier, inc=1, device_id=(peer, z), device_id_type=MESH)

    @pl.when(z > 0)
    def _():
        pl.semaphore_signal(barrier, inc=1, device_id=(f, z - 1), device_id_type=MESH)

    @pl.when(z < nz - 1)
    def _():
        pl.semaphore_signal(barrier, inc=1, device_id=(f, z + 1), device_id_type=MESH)

    beside = f - 1 + 2 * lax.rem(f, 2)

    @pl.when(jnp.logical_and(beside >= 0, beside < nf))
    def _():
        pl.semaphore_signal(barrier, inc=1, device_id=(beside, z), device_id_type=MESH)

    peers = (
        3
        + (z + nz - 1) // nz
        + (2 * nz - 2 - z) // nz
        + (f + nf - 1) // nf
        + (2 * nf - 2 - f) // nf
        - 1
    )
    pl.semaphore_wait(barrier, peers)

    def slot(p, origin, part):
        start, size = ((0, depth), (0, half), (half, half))[part]
        at = pl.ds(pl.multiple_of(origin * depth + start, half), size)
        return wbuf.at[p, at] if p < chunks else ofull_ref.at[at]

    def move(p, number, source, origin, part, peer):
        return pltpu.make_async_remote_copy(
            src_ref=source,
            dst_ref=slot(p, origin, part),
            send_sem=wsend.at[p, number],
            recv_sem=wrecv.at[p, number],
            device_id=(peer, z),
            device_id_type=MESH,
        )

    def sends(p):
        return [
            move(p, 0, slot(p, f, 0), f, 0, xn),
            move(p, 1, slot(p, f, 0), f, 0, yn),
            move(p, 2, slot(p, f, 0), f, 0, sib),
            move(p, 3, slot(p, xn, 1), xn, 1, yn),
            move(p, 4, slot(p, yn, 2), yn, 2, xn),
            move(p, 5, slot(p, xn, 0), xn, 0, sib),
            move(p, 6, slot(p, yn, 0), yn, 0, sib),
            move(p, 7, slot(p, dn, 1), dn, 1, sib),
            move(p, 8, slot(p, dn, 2), dn, 2, sib),
        ]

    def arrivals(p):
        where = [
            (xn, 0), (yn, 0), (sib, 0), (dn, 1), (dn, 2),
            (other(xn), 0), (other(yn), 0), (other(dn), 1), (other(dn), 2),
        ]
        return [
            pltpu.make_async_remote_copy(
                src_ref=slot(p, origin, part),
                dst_ref=slot(p, origin, part),
                send_sem=wsend.at[p, number],
                recv_sem=wrecv.at[p, number],
                device_id=(sib, z),
                device_id_type=MESH,
            )
            for number, (origin, part) in enumerate(where)
        ]

    out = [sends(p) for p in range(chunks + 1)]
    come = [arrivals(p) for p in range(chunks + 1)]

    def launch(p):
        if p <= chunks:
            for copy in local[p]:
                copy.wait()
            for number in (0, 1, 2):
                out[p][number].start()

    def spread(p):
        if p <= chunks:
            come[p][0].wait_recv()
            out[p][3].start()
            come[p][1].wait_recv()
            out[p][4].start()
            out[p][5].start()
            out[p][6].start()
            launch(p + 2)

    def spread_far(p):
        if p <= chunks:
            come[p][3].wait_recv()
            out[p][7].start()
            come[p][4].wait_recv()
            out[p][8].start()

    def ready(p):
        for number in (2, 5, 6, 7, 8):
            come[p][number].wait_recv()

    def hop(way, step):
        origin = z - step if way == 0 else z + step
        at = pl.ds(pl.multiple_of(origin * rows, rows), rows)
        return pltpu.make_async_remote_copy(
            src_ref=xbuf.at[at],
            dst_ref=xbuf.at[at],
            send_sem=tsend.at[way, step],
            recv_sem=trecv.at[way, step],
            device_id=(f, z + 1 if way == 0 else z - 1),
            device_id_type=MESH,
        )

    def sends_hop(way, step):
        if way == 0:
            return jnp.logical_and(z - step >= 0, z < nz - 1)
        return jnp.logical_and(z + step <= nz - 1, z > 0)

    def gets_hop(way, step):
        return z - 1 - step >= 0 if way == 0 else z + 1 + step <= nz - 1

    def start_hop(step):
        for way in (0, 1):
            @pl.when(sends_hop(way, step))
            def _():
                hop(way, step).start()

    def end_hop(step):
        for way in (0, 1):
            @pl.when(gets_hop(way, step))
            def _():
                origin = z - 1 - step if way == 0 else z + 1 + step
                at = pl.ds(pl.multiple_of(origin * rows, rows), rows)
                pltpu.make_async_remote_copy(
                    src_ref=xbuf.at[at],
                    dst_ref=xbuf.at[at],
                    send_sem=tsend.at[way, step],
                    recv_sem=trecv.at[way, step],
                    device_id=(f, z + 1 if way == 1 else z - 1),
                    device_id_type=MESH,
                ).wait_recv()

    def project(k):
        @pl.loop(0, 3)
        def _(branch):
            at = pl.ds(pl.multiple_of(branch * cw, cw), cw)
            pbuf[k, HALO : HALO + slab, at] = jnp.dot(
                xbuf[...], wbuf[k, :, at], preferred_element_type=jnp.float32
            ).astype(pbuf.dtype)

    def halo(k):
        return pltpu.make_async_remote_copy(
            src_ref=pbuf.at[k, pl.ds(slab, HALO)],
            dst_ref=pbuf.at[k, pl.ds(0, HALO)],
            send_sem=hsend.at[k],
            recv_sem=hrecv.at[k],
            device_id=(f + 1, z),
            device_id_type=MESH,
        )

    def send_halo(k):
        @pl.when(f < nf - 1)
        def _():
            halo(k).start()

    def get_halo(k):
        @pl.when(f > 0)
        def _():
            halo(k).wait_recv()

    ext = slab + 128

    def convolve(k):
        @pl.loop(0, cw // 128)
        def _(lane):
            lanes = pl.ds(pl.multiple_of(k * cw + lane * 128, 128), 128)
            for branch in range(3):
                source = pl.ds(pl.multiple_of(branch * cw + lane * 128, 128), 128)
                fbuf[branch] = pbuf[k, :, source].astype(jnp.float32)

            def short(branch, first, count):
                total = jnp.zeros((count, 128), jnp.float32)
                place = pos_ref[pl.ds(first, count), :]
                for tap in range(3):
                    weight = taps_ref[tap, pl.ds(branch, 1), lanes]
                    window = fbuf[branch, pl.ds(first - tap, count), :]
                    total = total + jnp.where(place >= tap, weight * window, 0.0)
                return total

            for block in range(ext // 128):
                first = HALO - 128 + block * 128
                product = short(1, first, 128) * short(2, first, 128)
                kvbuf[pl.ds(block * 128, 128), :] = product.astype(jnp.bfloat16).astype(
                    jnp.float32
                )
            for shift in range(16):
                shbuf[shift, pl.ds(16, ext - 16), :] = kvbuf[
                    pl.ds(16 - shift, ext - 16), :
                ].astype(jnp.bfloat16)

            for block in range(slab // 128):
                first = (
                    jnp.minimum(pos_ref[pl.ds(HALO + block * 128, 128), :], 128)
                    .astype(jnp.float32)
                    .astype(jnp.bfloat16)
                    .reshape(8, 16, 128)
                )

                def taps(group, carried):
                    place, total = carried
                    weights = shaped_ref[pl.ds(pl.multiple_of(group * 16, 16), 16), lanes]
                    start = pl.multiple_of(128 + block * 128 - group * 16, 16)
                    for first_shift in (0, 8):
                        few = jnp.zeros((8, 16, 128), jnp.bfloat16)
                        for shift in range(first_shift, first_shift + 8):
                            window = shbuf[shift, pl.ds(start, 128), :].reshape(8, 16, 128)
                            weight = jnp.broadcast_to(
                                weights[shift : shift + 1, :], (16, 128)
                            ).astype(jnp.bfloat16)
                            few = few + jnp.where(
                                place >= jnp.bfloat16(shift),
                                weight[None] * window,
                                jnp.bfloat16(0.0),
                            )
                        total = total + few.astype(jnp.float32)
                    return place - jnp.bfloat16(16.0), total

                _, mixed = lax.fori_loop(
                    0, 8, taps, (first, jnp.zeros((8, 16, 128), jnp.float32))
                )
                mixed = mixed.reshape(128, 128)
                query = short(0, HALO + block * 128, 128)
                gated_ref[pl.ds(block * 128, 128), lanes] = (query * mixed).astype(
                    jnp.bfloat16
                )

    columns = 2 * depth
    pairs = [f // 2, xn // 2, yn // 2, dn // 2]

    def part(owner, q):
        at = pl.ds(pl.multiple_of(pairs[q] * columns, columns), columns)
        return lax.dot_general(
            gated_ref[pl.ds(pl.multiple_of(owner * rows, rows), rows), :],
            ofull_ref[at, :],
            (((1,), (1,)), ((), ())),
            preferred_element_type=jnp.float32,
        )

    def carry(way, step, q):
        return pltpu.make_async_remote_copy(
            src_ref=rbuf.at[way, step, q],
            dst_ref=rbuf.at[way, step, q],
            send_sem=rsend.at[way, step, q],
            recv_sem=rrecv.at[way, step, q],
            device_id=(f, z + 1 if way == 0 else z - 1),
            device_id_type=MESH,
        )

    def arrive(way, step, q):
        pltpu.make_async_remote_copy(
            src_ref=rbuf.at[way, step, q],
            dst_ref=rbuf.at[way, step, q],
            send_sem=rsend.at[way, step, q],
            recv_sem=rrecv.at[way, step, q],
            device_id=(f, z - 1 if way == 0 else z + 1),
            device_id_type=MESH,
        ).wait_recv()

    def carries(way, step):
        return nz - 1 - step > z if way == 0 else step < z

    def has_before(way):
        return z > 0 if way == 0 else z < nz - 1

    def pass_sums(q):
        for step in range(3):
            for way in (0, 1):
                owner = 3 - step if way == 0 else step

                @pl.when(carries(way, step))
                def _():
                    value = part(owner, q)

                    @pl.when(has_before(way))
                    def _():
                        arrive(way, step, q)
                        rbuf[way, step, q] = (
                            value + rbuf[way, step, q].astype(jnp.float32)
                        ).astype(jnp.bfloat16)

                    @pl.when(jnp.logical_not(has_before(way)))
                    def _():
                        rbuf[way, step, q] = value.astype(jnp.bfloat16)

                    carry(way, step, q).start()

    def settle(q):
        at = pl.ds(pl.multiple_of(pairs[q] * columns, columns), columns)
        sums[...] = part(z, q) + x_ref[:, at].astype(jnp.float32)
        for step in range(3):
            for way in (0, 1):
                here = z == nz - 1 - step if way == 0 else z == step

                @pl.when(here)
                def _():
                    arrive(way, step, q)
                    sums[...] = sums[...] + rbuf[way, step, q].astype(jnp.float32)

        out_ref[:, at] = sums[...].astype(jnp.bfloat16)

    start_hop(0)
    launch(0)
    launch(1)
    spread(0)
    end_hop(0)
    start_hop(1)
    spread_far(0)
    spread(1)
    end_hop(1)
    start_hop(2)
    spread_far(1)
    spread(2)
    end_hop(2)
    ready(0)
    project(0)
    send_halo(0)
    spread_far(2)
    ready(1)
    project(1)
    send_halo(1)
    get_halo(0)
    convolve(0)
    spread(3)
    ready(2)
    project(2)
    send_halo(2)
    get_halo(1)
    convolve(1)
    spread_far(3)
    ready(3)
    project(3)
    send_halo(3)
    get_halo(2)
    convolve(2)
    spread(4)
    get_halo(3)
    convolve(3)
    come[chunks][2].wait_recv()
    pass_sums(0)
    spread_far(4)
    come[chunks][5].wait_recv()
    pass_sums(1)
    settle(0)
    come[chunks][6].wait_recv()
    pass_sums(2)
    settle(1)
    come[chunks][7].wait_recv()
    come[chunks][8].wait_recv()
    pass_sums(3)
    settle(2)
    settle(3)

    for step in range(3):
        for way in (0, 1):
            @pl.when(carries(way, step))
            def _():
                for q in range(4):
                    carry(way, step, q).wait_send()

    for p in range(chunks + 1):
        for copy in out[p]:
            copy.wait_send()
    for step in range(3):
        for way in (0, 1):
            @pl.when(sends_hop(way, step))
            def _():
                hop(way, step).wait_send()

    @pl.when(f < nf - 1)
    def _():
        for k in range(chunks):
            halo(k).wait_send()


def body(tokens, in_weight, out_weight, short_taps, filter_taps, decay_rate, doc_lengths):
    rows, model = tokens.shape
    depth, _, channels = in_weight.shape
    slab = rows * lax.axis_size("tp")
    nf = lax.axis_size("fsdp")
    chunks = 4
    cw = channels // chunks
    vmem = pl.BlockSpec(memory_space=pltpu.VMEM)
    anywhere = pl.BlockSpec(memory_space=pl.ANY)
    return pl.pallas_call(
        mix_kernel,
        out_shape=jax.ShapeDtypeStruct((rows, model), jnp.bfloat16),
        in_specs=[
            pl.BlockSpec(memory_space=pltpu.SMEM), vmem, anywhere, anywhere, vmem, vmem, vmem,
        ],
        out_specs=vmem,
        scratch_shapes=[
            pltpu.VMEM((slab, channels), jnp.bfloat16),
            pltpu.VMEM((nf * depth, channels), jnp.bfloat16),
            pltpu.VMEM(filter_taps.shape, jnp.float32),
            pltpu.VMEM((slab + HALO, 128), jnp.int32),
            pltpu.VMEM((chunks, nf * depth, 3 * cw), jnp.bfloat16),
            pltpu.VMEM((slab, model), jnp.bfloat16),
            pltpu.VMEM((chunks, slab + HALO, 3 * cw), jnp.bfloat16),
            pltpu.VMEM((3, slab + HALO, 128), jnp.float32),
            pltpu.VMEM((slab + 128, 128), jnp.float32),
            pltpu.VMEM((16, slab + 128, 128), jnp.bfloat16),
            pltpu.VMEM((2, 3, 4, rows, 2 * depth), jnp.bfloat16),
            pltpu.VMEM((rows, 2 * depth), jnp.float32),
            pltpu.SemaphoreType.DMA((chunks + 1, 9)),
            pltpu.SemaphoreType.DMA((chunks + 1, 9)),
            pltpu.SemaphoreType.DMA((2, 3)),
            pltpu.SemaphoreType.DMA((2, 3)),
            pltpu.SemaphoreType.DMA((chunks,)),
            pltpu.SemaphoreType.DMA((chunks,)),
            pltpu.SemaphoreType.DMA((chunks + 1, 3)),
            pltpu.SemaphoreType.DMA((2, 3, 4)),
            pltpu.SemaphoreType.DMA((2, 3, 4)),
        ],
        compiler_params=pltpu.CompilerParams(
            collective_id=0, has_side_effects=True, vmem_limit_bytes=62 * 1024 * 1024
        ),
        cost_estimate=pl.CostEstimate(
            flops=2 * slab * model * 4 * channels,
            bytes_accessed=16 * 1024 * 1024,
            transcendentals=0,
        ),
    )(
        doc_lengths,
        tokens,
        in_weight.transpose(1, 0, 2),
        out_weight,
        short_taps,
        filter_taps,
        decay_rate[None, :],
    )


def solution(mesh):
    in_specs = (
        P(("fsdp", "tp"), None),
        P("fsdp", None, "tp"),
        P("fsdp", "tp"),
        P(None, None, "tp"),
        P(None, "tp"),
        P("tp"),
        P(),
    )
    out_specs = P(("fsdp", "tp"), None)
    small = mesh.shape["fsdp"] == 8 and mesh.shape["tp"] == 4
    return jax.shard_map(
        body if small else general_body,
        mesh=mesh,
        in_specs=in_specs,
        out_specs=out_specs,
        check_vma=False,
    )
```
